32 devices in a mesh: row: 16 (over z, y, core), col: 2 (over x).
Axes of the slice: x: 2, y: 2, z: 4, core: 2. Of those that a mesh axis runs over, the one named last changes fastest.
Arguments:
- kernel: float32 [4096, 4096], P('row', 'col')
- targets: float32 [4096, 64], P('row'), may hold values from -60 to 60
Outputs:
- schur: float32 [4096, 4096], P('row', 'col')
- factor: float32 [4096, 512], P('row')
- solved: float32 [4096, 64], P('row')
The draws below stay inside these ranges and needn't reach their ends.
All inputs are finite; a program needn't handle non-finite values.
Results may differ from the reference program's by a relative error of at most 0.00022.
Values sent between devices are 32-bit elements; how exact they have to be, the bound alone decides.
A program may use at most 64 MiB of HBM per device.

```python
import jax
import jax.numpy as jnp
from jax import lax

NB = 256
RHS = 64
PANELS = 2
N = 4096
CB = 8


centre_dims = 24


ridge_rate = 0.001


def draw_kernel(key, part):
    first = jax.random.fold_in(key, 11)
    centres = jax.random.normal(first, (N, centre_dims), jnp.float32)
    centres = centres - jnp.mean(centres, axis=0)[None, :]
    spacing = 2.0 * jnp.sum(jnp.mean(centres * centres, axis=0))
    norms = jnp.sum(centres * centres, axis=1)
    gram = jnp.dot(centres, centres.T, precision=lax.Precision.HIGHEST)
    distance = jnp.maximum(norms[:, None] + norms[None, :] - 2.0 * gram, jnp.float32(0.0))
    matrix = jnp.exp(-distance / (2.0 * spacing))
    matrix = (matrix + matrix.T) * 0.5
    on_diag = jnp.arange(N)[:, None] == jnp.arange(N)[None, :]
    matrix = jnp.where(on_diag, jnp.float32(1.0 + ridge_rate * N), matrix)
    grid_cols = N // (NB * CB)
    return matrix.reshape(N, CB, grid_cols, NB).transpose(0, 2, 1, 3).reshape(N, N)


def block_levels(own_key, dims, split, least, top_value):
    gain, own = 1.0, jax.random.fold_in(own_key, 6)
    for position, parts in split:
        steps = jnp.exp(jax.random.uniform(jax.random.fold_in(own, position), (parts,), jnp.float32, least / len(split), top_value / len(split)))
        gain = gain * jnp.repeat(steps, dims[position] // parts).reshape([-1 if axis == position else 1 for axis in range(len(dims))])
    return gain


def centred(rng, extent, deviation, limit, shards=(), kind=jnp.bfloat16):
    entries = jax.random.normal(rng, extent, jnp.float32) * deviation
    if len(shards) > 0:
        entries = block_levels(rng, extent, shards, -0.22, 0.18) * entries
    return jnp.clip(entries, min=-limit, max=limit).astype(kind)


def setup_inputs(seed: int = 0) -> dict:
    key_list = jax.random.split(jax.random.key(seed), 3)
    return {
        "kernel": draw_kernel(jax.random.fold_in(key_list[2], 71), 0),
        "targets": centred(key_list[1], (N, RHS), 10.0, 60.0, ((0, 16),), jnp.float32),
    }


def reference(kernel, targets):
    grid_cols = N // (NB * CB)
    matrix = kernel.reshape(N, grid_cols, CB, NB).transpose(0, 2, 1, 3).reshape(N, N)
    rhs_now = targets
    block_ids = jnp.arange(N, dtype=jnp.int32) // NB
    columns_out = []
    for step in range(PANELS):
        start = step * NB
        lower = jnp.linalg.cholesky(matrix[start:start + NB, start:start + NB])
        column = matrix[:, start:start + NB]
        panel = lax.linalg.triangular_solve(lower, column, left_side=False, lower=True, transpose_a=True)
        panel = jnp.where((block_ids > step)[:, None], panel, jnp.float32(0.0))
        top = lax.linalg.triangular_solve(lower, rhs_now[start:start + NB], left_side=True, lower=True)
        rhs_now = rhs_now - jnp.dot(panel, top, precision=lax.Precision.HIGHEST)
        rhs_now = rhs_now.at[start:start + NB].set(top)
        columns_out.append(panel.at[start:start + NB].set(lower))
        row_blocks = matrix.reshape(N // NB, NB, N)
        panel_blocks = panel.reshape(N // NB, NB, NB)

        def update(pair):
            return pair[0] - jnp.dot(pair[1], panel.T, precision=lax.Precision.HIGHEST)
        matrix = lax.map(update, (row_blocks, panel_blocks)).reshape(N, N)
    schur = matrix.reshape(N, CB, grid_cols, NB).transpose(0, 2, 1, 3).reshape(N, N)
    return (schur, jnp.concatenate(columns_out, axis=1), rhs_now)
```

```python
import functools

import jax
import jax.numpy as jnp
from jax import lax
from jax.experimental import pallas as pl
from jax.experimental.pallas import tpu as pltpu
from jax.sharding import PartitionSpec as P

PANELS = 2
TILE = 128
F32 = jnp.float32
HIGHEST = lax.Precision.HIGHEST
NN = (((1,), (0,)), ((), ()))
NT = (((1,), (1,)), ((), ()))
TN = (((0,), (0,)), ((), ()))


def dot(a, b, dims):
    return lax.dot_general(a, b, dims, precision=HIGHEST, preferred_element_type=F32)


def split(a):
    high = a.astype(jnp.bfloat16)
    return high, (a - high.astype(F32)).astype(jnp.bfloat16)


def dot3(a, b, dims):
    (ah, al), (bh, bl) = a, b
    one = functools.partial(lax.dot_general, dimension_numbers=dims, preferred_element_type=F32)
    return one(ah, bh) + (one(ah, bl) + one(al, bh))


def eliminate(block):
    n = block.shape[0]
    lane = lax.broadcasted_iota(jnp.int32, (8, n), 1)
    sub = lax.broadcasted_iota(jnp.int32, (8, n), 0)
    tiles = [block[8 * t : 8 * t + 8] for t in range(n // 8)]

    def wide(x):
        return jnp.broadcast_to(x, (8, n))

    for p in range(0, n, 2):
        q, g, s = p + 1, p // 8, p % 8
        row_p = wide(tiles[g][s : s + 1])
        row_q = wide(tiles[g][s + 1 : s + 2])
        a, b, d = wide(row_p[:, p : p + 1]), wide(row_p[:, q : q + 1]), wide(row_q[:, q : q + 1])
        inv_a = 1.0 / a
        inv_q = a * (1.0 / (a * d - b * b))
        ratio = b * inv_a
        at_p, at_q = lane == p, lane == q
        pair = at_p | at_q
        new_q = jnp.where(at_p, -ratio, row_q - ratio * row_p)
        use_p = jnp.where(at_p, 1.0, jnp.where(at_q, 0.0, row_p))
        use_q = jnp.where(at_q, 1.0, new_q)
        for t in range(g, n // 8):
            col_p, col_q = wide(tiles[t][:, p : p + 1]), wide(tiles[t][:, q : q + 1])
            m_p = col_p * inv_a
            m_q = (col_q - m_p * b) * inv_q
            new = jnp.where(pair, 0.0, tiles[t]) - m_p * use_p - m_q * use_q
            if t == g:
                new = jnp.where(sub > s + 1, new, jnp.where(sub == s + 1, new_q, tiles[t]))
            tiles[t] = new
    return jnp.concatenate(tiles, axis=0)


def factorise(work):
    n = work.shape[0]
    rows = lax.broadcasted_iota(jnp.int32, (TILE, TILE), 0)
    cols = lax.broadcasted_iota(jnp.int32, (TILE, TILE), 1)
    row_id = lax.broadcasted_iota(jnp.int32, (n, n), 0)
    col_id = lax.broadcasted_iota(jnp.int32, (n, n), 1)
    lane = lax.broadcasted_iota(jnp.int32, (TILE, n), 1)

    def body(k, carry):
        at = pl.multiple_of(k * TILE, TILE)
        done = eliminate(work[pl.ds(at, TILE), pl.ds(at, TILE)])
        pivots = jnp.sum(jnp.where(rows == cols, done, 0.0), axis=1, keepdims=True)
        scale = 1.0 / jnp.sqrt(pivots)
        inverse = scale * jnp.where(rows > cols, done, jnp.where(rows == cols, 1.0, 0.0))
        work[pl.ds(at, TILE), :] = dot(inverse, work[pl.ds(at, TILE), :], NN)
        work[pl.ds(at, TILE), pl.ds(at, TILE)] = inverse
        strip = work[pl.ds(at, TILE), :]
        later = jnp.where(lane >= at + TILE, strip, 0.0)
        below = row_id >= at + TILE
        here = (col_id >= at) & (col_id < at + TILE)
        work[...] = jnp.where(below & here, 0.0, work[...]) - dot(later, strip, TN)
        return carry

    lax.fori_loop(0, n // TILE, body, 0)


def finish(my_row, my_col, work, own, head_rhs, matrix, rhs, gathered, out, factor, solved):
    block = matrix.shape[0]
    width = own.shape[1]
    row_id = lax.broadcasted_iota(jnp.int32, (width, width), 0)
    col_id = lax.broadcasted_iota(jnp.int32, (width, width), 1)
    inverse = jnp.where(row_id >= col_id, work[...], 0.0)
    rows = lax.broadcasted_iota(jnp.int32, (block, width), 0) + my_row * block
    cols = lax.broadcasted_iota(jnp.int32, (block, width), 1)
    panel = jnp.where(cols <= rows, dot(own[...], inverse, NT), 0.0)
    factor[...] = panel
    panel = jnp.where(cols < my_row * block, panel, 0.0)
    top = dot(inverse, head_rhs[...], NN)
    value = rhs[...] - dot(panel, top, NN)
    for k in range(width // block):
        value = jnp.where(my_row == k, top[k * block : (k + 1) * block], value)
    solved[...] = value
    weight = dot(panel, inverse, NN)
    first = jnp.where(my_col == 0, 0.0, weight)
    for k in range(1, width // block):
        part = dot(jnp.where(cols < k * block, panel, 0.0), inverse, NN)
        first = jnp.where(my_col == k, part, first)
    first, weight = split(first), split(weight)
    for m in range(matrix.shape[1] // block):
        here = slice(m * block, (m + 1) * block)
        other = split(gathered[m])
        out[:, here] = matrix[:, here] - dot3(first if m == 0 else weight, other, NT)


def local_kernel(head, own, head_rhs, matrix, rhs, gathered, out, factor, solved, work):
    work[...] = head[...]
    factorise(work)
    finish(
        lax.axis_index("row"), lax.axis_index("col"),
        work, own, head_rhs, matrix, rhs, gathered, out, factor, solved,
    )


def gather(matrix, targets):
    block = matrix.shape[0]
    mine = lax.axis_index("col")
    pieces = lax.all_gather(matrix[:, :block], "col", axis=0)
    own = jnp.concatenate([pieces[k] for k in range(PANELS)], axis=1)
    every = lax.all_gather(own, "row", axis=0)
    head = every[:PANELS].reshape(PANELS * block, PANELS * block)
    grid_cols = lax.axis_size("col")
    every = every.reshape(-1, grid_cols, block, PANELS * block)
    gathered = lax.dynamic_index_in_dim(every, mine, 1, keepdims=False)
    return head, own, gathered


def head_of(targets):
    my_row = lax.axis_index("row")
    kept = jnp.concatenate(
        [jnp.where(my_row == k, targets, F32(0.0)) for k in range(PANELS)], axis=0
    )
    return lax.psum(kept, "row")


def shards(matrix, targets):
    head_rhs = head_of(targets)
    head, own, gathered = gather(matrix, targets)
    block = matrix.shape[0]
    width = PANELS * block
    vmem = pl.BlockSpec(memory_space=pltpu.VMEM)
    return pl.pallas_call(
        local_kernel,
        out_shape=(
            jax.ShapeDtypeStruct(matrix.shape, F32),
            jax.ShapeDtypeStruct((block, width), F32),
            jax.ShapeDtypeStruct(targets.shape, F32),
        ),
        in_specs=[vmem] * 6,
        out_specs=(vmem, vmem, vmem),
        scratch_shapes=[pltpu.VMEM((width, width), F32)],
        compiler_params=pltpu.CompilerParams(vmem_limit_bytes=48 * 1024 * 1024),
    )(head, own, head_rhs, matrix, targets, gathered)


def solution(mesh):
    return jax.shard_map(
        shards,
        mesh=mesh,
        in_specs=(P("row", "col"), P("row", None)),
        out_specs=(P("row", "col"), P("row", None), P("row", None)),
        check_vma=False,
    )
```

```python
import functools

import jax
import jax.numpy as jnp
from jax import lax
from jax.experimental import pallas as pl
from jax.experimental.pallas import tpu as pltpu
from jax.sharding import PartitionSpec as P

PANELS = 2
TILE = 128
F32 = jnp.float32
HIGHEST = lax.Precision.HIGHEST
NN = (((1,), (0,)), ((), ()))
NT = (((1,), (1,)), ((), ()))
TN = (((0,), (0,)), ((), ()))


def dot(a, b, dims):
    return lax.dot_general(a, b, dims, precision=HIGHEST, preferred_element_type=F32)


def split(a):
    high = a.astype(jnp.bfloat16)
    return high, (a - high.astype(F32)).astype(jnp.bfloat16)


def dot3(a, b, dims):
    (ah, al), (bh, bl) = a, b
    one = functools.partial(lax.dot_general, dimension_numbers=dims, preferred_element_type=F32)
    return one(ah, bh) + (one(ah, bl) + one(al, bh))


def eliminate(block):
    n = block.shape[0]
    lane = lax.broadcasted_iota(jnp.int32, (8, n), 1)
    sub = lax.broadcasted_iota(jnp.int32, (8, n), 0)
    tiles = [block[8 * t : 8 * t + 8] for t in range(n // 8)]

    def wide(x):
        return jnp.broadcast_to(x, (8, n))

    for p in range(0, n, 2):
        q, g, s = p + 1, p // 8, p % 8
        row_p = wide(tiles[g][s : s + 1])
        row_q = wide(tiles[g][s + 1 : s + 2])
        a, b, d = wide(row_p[:, p : p + 1]), wide(row_p[:, q : q + 1]), wide(row_q[:, q : q + 1])
        inv_a = 1.0 / a
        inv_q = a * (1.0 / (a * d - b * b))
        ratio = b * inv_a
        at_p, at_q = lane == p, lane == q
        pair = at_p | at_q
        new_q = jnp.where(at_p, -ratio, row_q - ratio * row_p)
        use_p = jnp.where(at_p, 1.0, jnp.where(at_q, 0.0, row_p))
        use_q = jnp.where(at_q, 1.0, new_q)
        for t in range(g, n // 8):
            col_p, col_q = wide(tiles[t][:, p : p + 1]), wide(tiles[t][:, q : q + 1])
            m_p = col_p * inv_a
            m_q = (col_q - m_p * b) * inv_q
            new = jnp.where(pair, 0.0, tiles[t]) - m_p * use_p - m_q * use_q
            if t == g:
                new = jnp.where(sub > s + 1, new, jnp.where(sub == s + 1, new_q, tiles[t]))
            tiles[t] = new
    return jnp.concatenate(tiles, axis=0)


def factorise(work, between):
    n = work.shape[0]
    rows = lax.broadcasted_iota(jnp.int32, (TILE, TILE), 0)
    cols = lax.broadcasted_iota(jnp.int32, (TILE, TILE), 1)
    row_id = lax.broadcasted_iota(jnp.int32, (n, n), 0)
    col_id = lax.broadcasted_iota(jnp.int32, (n, n), 1)
    lane = lax.broadcasted_iota(jnp.int32, (TILE, n), 1)

    for k in range(n // TILE):
        at = k * TILE
        done = eliminate(work[pl.ds(at, TILE), pl.ds(at, TILE)])
        pivots = jnp.sum(jnp.where(rows == cols, done, 0.0), axis=1, keepdims=True)
        scale = 1.0 / jnp.sqrt(pivots)
        inverse = scale * jnp.where(rows > cols, done, jnp.where(rows == cols, 1.0, 0.0))
        work[pl.ds(at, TILE), :] = dot(inverse, work[pl.ds(at, TILE), :], NN)
        work[pl.ds(at, TILE), pl.ds(at, TILE)] = inverse
        strip = work[pl.ds(at, TILE), :]
        later = jnp.where(lane >= at + TILE, strip, 0.0)
        below = row_id >= at + TILE
        here = (col_id >= at) & (col_id < at + TILE)
        work[...] = jnp.where(below & here, 0.0, work[...]) - dot(later, strip, TN)
        between(k)


def finish(my_row, my_col, work, own, head, head_rhs, matrix, rhs, gathered, out, factor, solved):
    block = matrix.shape[0]
    width = own.shape[1]
    row_id = lax.broadcasted_iota(jnp.int32, (width, width), 0)
    col_id = lax.broadcasted_iota(jnp.int32, (width, width), 1)
    inverse = jnp.where(row_id >= col_id, work[...], 0.0)
    rows = lax.broadcasted_iota(jnp.int32, (block, width), 0) + my_row * block
    cols = lax.broadcasted_iota(jnp.int32, (block, width), 1)
    panel = jnp.where(cols <= rows, dot(own[...], inverse, NT), 0.0)
    factor[...] = panel
    panel = jnp.where(cols < my_row * block, panel, 0.0)
    top = dot(inverse, head_rhs[...], NN)
    value = rhs[...] - dot(panel, top, NN)
    for k in range(width // block):
        value = jnp.where(my_row == k, top[k * block : (k + 1) * block], value)
    solved[...] = value
    weight = dot(panel, inverse, NN)
    first = jnp.where(my_col == 0, 0.0, weight)
    for k in range(1, width // block):
        part = dot(jnp.where(cols < k * block, panel, 0.0), inverse, NN)
        first = jnp.where(my_col == k, part, first)
    first, weight = split(first), split(weight)
    for m in range(matrix.shape[1] // block):
        here = slice(m * block, (m + 1) * block)
        other = gathered[m]
        if m == 0 and head is not None:
            other = head[pl.ds(pl.multiple_of(my_col * block, block), block), :]
        other = split(other)
        out[:, here] = matrix[:, here] - dot3(first if m == 0 else weight, other, NT)


def local_kernel(head, own, head_rhs, matrix, rhs, gathered, out, factor, solved, work):
    work[...] = head[...]
    factorise(work, lambda k: None)
    finish(
        lax.axis_index("row"), lax.axis_index("col"),
        work, own, None, head_rhs, matrix, rhs, gathered, out, factor, solved,
    )


CHUNKS = 4
MESH = pl.DeviceIdType.MESH


def fused_kernel(
    matrix, rhs, out, factor, solved, work, own, head, head_rhs, gathered,
    head_send, head_recv, ring_send, ring_recv, core_send, core_recv, swap_send, swap_recv,
):
    block = matrix.shape[0]
    half, chunk = block // 2, block // CHUNKS
    my_row, col = lax.axis_index("row"), lax.axis_index("col")
    chips = lax.axis_size("row") // 2
    far = chips // 2
    chip, core = my_row // 2, lax.rem(my_row, 2)

    def chip_at(place):
        return jnp.where(place < far, 2 * place, 2 * (chips - 1 - place) + 1)

    place = jnp.where(lax.rem(chip, 2) == 0, chip // 2, chips - 1 - chip // 2)
    right = (2 * chip_at(lax.rem(place + 1, chips)) + core, col)
    left = (2 * chip_at(lax.rem(place + chips - 1, chips)) + core, col)
    sibling = (2 * chip + 1 - core, col)
    across = (my_row, 1 - col)
    cross = (2 * chip + 1 - core, 1 - col)

    def copy(src, dst, send, recv, device):
        return pltpu.make_async_remote_copy(
            src_ref=src, dst_ref=dst, send_sem=send, recv_sem=recv,
            device_id=device, device_id_type=MESH,
        )

    def when(condition, action):
        pl.when(condition)(action)

    def panel_at(index):
        return pl.ds(pl.multiple_of(index * block, block), block)

    def rows_at(index, size):
        return pl.ds(pl.multiple_of(index * size, size), size)

    barrier = pltpu.get_barrier_semaphore()
    for device in (right, left, sibling, across, cross):
        pl.semaphore_signal(barrier, inc=1, device_id=device, device_id_type=MESH)
    pl.semaphore_wait(barrier, 5)

    def head_part(i, on_core, on_col):
        if i == CHUNKS:
            return head_rhs.at[panel_at(on_core), :]
        return head.at[
            pl.ds(pl.multiple_of(on_core * block + i * chunk, chunk), chunk), panel_at(on_col)
        ]

    def head_copy(kind, i, device, on_core, on_col):
        part = head_part(i, on_core, on_col)
        return copy(part, part, head_send.at[kind, i], head_recv.at[kind, i], device)

    def head_right(i):
        part = head_part(i, core, col)
        return copy(part, part, head_send.at[0, i], head_recv.at[0, i], right)

    def head_left(i):
        part = head_part(i, core, col)
        return copy(part, part, head_send.at[1, i], head_recv.at[0, i], left)

    sends_right = place < far
    sends_left = (place == 0) | (place > far + 1)

    @pl.when(place == 0)
    def _():
        head[panel_at(core), panel_at(col)] = matrix[:, :block]
        head_rhs[panel_at(core), :] = rhs[...]

    own[:, panel_at(col)] = matrix[:, :block]
    mine = core == col

    def swap_same():
        here = rows_at(1 - core, half)
        return copy(
            matrix.at[here, pl.ds(0, block)],
            gathered.at[chip, here, panel_at(col)],
            swap_send.at[0], swap_recv.at[0], sibling,
        )

    def swap_over(kind, to_core, device):
        here = rows_at(to_core, half)
        return copy(
            matrix.at[here, pl.ds(0, block)],
            gathered.at[chip, here, panel_at(col)],
            swap_send.at[kind], swap_recv.at[1], device,
        )

    own_copy = copy(
        matrix.at[:, pl.ds(0, block)], own.at[:, panel_at(col)], swap_send.at[3], swap_recv.at[3], across
    )

    for i in range(CHUNKS + 1):
        when(place > 0, lambda i=i: head_right(i).wait_recv())
        when(sends_right, lambda i=i: head_right(i).start())
        when(sends_left, lambda i=i: head_left(i).start())
        if i < CHUNKS:
            head_copy(2, i, across, core, col).start()
        head_copy(3, i, sibling, core, col).start()

    @pl.when(mine)
    def _():
        here = rows_at(core, half)
        gathered[chip, here, panel_at(col)] = matrix[here, :block]
        swap_same().start()

    @pl.when(jnp.logical_not(mine))
    def _():
        swap_over(1, core, across).start()
        swap_over(2, 1 - core, cross).start()

    for i in range(CHUNKS):
        part = head_part(i, core, 1 - col)
        copy(part, part, head_send.at[2, i], head_recv.at[2, i], across).wait_recv()
        head_copy(4, i, sibling, core, 1 - col).start()
    own_copy.start()
    for i in range(CHUNKS):
        for kind, on_col in ((3, col), (4, 1 - col)):
            part = head_part(i, 1 - core, on_col)
            copy(part, part, head_send.at[kind, i], head_recv.at[kind, i], sibling).wait_recv()
    work[...] = head[...]

    def piece(origin, on_core, part=None):
        start, size = on_core * half, half
        if part is not None:
            start, size = start + part * (half // 2), half // 2
        return gathered.at[chip_at(origin), pl.ds(pl.multiple_of(start, size), size), :]

    def origin(direction, step):
        return lax.rem(place + (chips - step if direction == 0 else step), chips)

    def ring_copy(direction, step, source):
        part = direction if step == far else None
        ref = piece(source, core, part)
        return copy(
            ref, ref, ring_send.at[direction, step], ring_recv.at[direction, step],
            left if direction else right,
        )

    def core_copy(index, source, on_core):
        ref = piece(source, on_core)
        return copy(ref, ref, core_send.at[index], core_recv.at[index], sibling)

    def ring_start(step):
        for direction in range(2):
            source = origin(direction, step - 1)
            when(source > 0, lambda d=direction, o=source: ring_copy(d, step, o).start())

    arrivals = [(0, place)] + [
        (1 + direction * (far - 1) + step - 1, origin(direction, step))
        for direction in range(2) for step in range(1, far)
    ] + [(2 * far - 1, origin(0, far))]

    def ring_step(step):
        for direction in range(2):
            source = origin(direction, step)
            when(source > 0, lambda d=direction, o=source: ring_copy(d, step, o).wait_recv())
        if step < far:
            ring_start(step + 1)
            for direction in range(2):
                source = origin(direction, step)
                index = 1 + direction * (far - 1) + step - 1
                when(source > 0, lambda n=index, o=source: core_copy(n, o, core).start())
        else:
            source = origin(0, far)
            when(source > 0, lambda: core_copy(2 * far - 1, source, core).start())

    when(jnp.logical_not(mine), lambda: swap_same().wait_recv())
    swap_over(1, core, across).wait_recv()
    ring_start(1)
    when(place > 0, lambda: core_copy(0, place, core).start())

    steps = work.shape[0] // TILE
    factorise(work, lambda k: [ring_step(s) for s in range(1, far + 1) if min(s, steps) == k + 1])

    for index, source in arrivals:
        when(source > 0, lambda n=index, o=source: core_copy(n, o, 1 - core).wait_recv())
    own_copy.wait_recv()
    part = head_part(CHUNKS, 1 - core, col)
    copy(part, part, head_send.at[3, CHUNKS], head_recv.at[3, CHUNKS], sibling).wait_recv()

    finish(my_row, col, work, own, head, head_rhs, matrix, rhs, gathered, out, factor, solved)

    for i in range(CHUNKS + 1):
        when(sends_right, lambda i=i: head_right(i).wait_send())
        when(sends_left, lambda i=i: head_left(i).wait_send())
        head_copy(3, i, sibling, core, col).wait_send()
        if i < CHUNKS:
            head_copy(2, i, across, core, col).wait_send()
            head_copy(4, i, sibling, core, 1 - col).wait_send()
    when(mine, lambda: swap_same().wait_send())
    for kind, to_core, device in ((1, core, across), (2, 1 - core, cross)):
        when(jnp.logical_not(mine), lambda k=kind, t=to_core, d=device: swap_over(k, t, d).wait_send())
    own_copy.wait_send()
    for step in range(1, far + 1):
        for direction in range(2):
            source = origin(direction, step - 1)
            when(source > 0, lambda d=direction, s=step, o=source: ring_copy(d, s, o).wait_send())
    for index, source in arrivals:
        when(source > 0, lambda n=index, o=source: core_copy(n, o, core).wait_send())


def fused(matrix, targets):
    block = matrix.shape[0]
    width = PANELS * block
    chips = lax.axis_size("row") // 2
    vmem = pl.BlockSpec(memory_space=pltpu.VMEM)
    dma = pltpu.SemaphoreType.DMA
    return pl.pallas_call(
        fused_kernel,
        out_shape=(
            jax.ShapeDtypeStruct(matrix.shape, F32),
            jax.ShapeDtypeStruct((block, width), F32),
            jax.ShapeDtypeStruct(targets.shape, F32),
        ),
        in_specs=[vmem] * 2,
        out_specs=(vmem, vmem, vmem),
        scratch_shapes=[
            pltpu.VMEM((width, width), F32),
            pltpu.VMEM((block, width), F32),
            pltpu.VMEM((width, width), F32),
            pltpu.VMEM((width, targets.shape[1]), F32),
            pltpu.VMEM((chips, block, width), F32),
            dma((5, CHUNKS + 1)), dma((5, CHUNKS + 1)),
            dma((2, chips // 2 + 1)), dma((2, chips // 2 + 1)),
            dma((chips,)), dma((chips,)),
            dma((4,)), dma((4,)),
        ],
        compiler_params=pltpu.CompilerParams(
            vmem_limit_bytes=48 * 1024 * 1024, collective_id=0, has_side_effects=True
        ),
    )(matrix, targets)


def gather(matrix, targets):
    block = matrix.shape[0]
    mine = lax.axis_index("col")
    pieces = lax.all_gather(matrix[:, :block], "col", axis=0)
    own = jnp.concatenate([pieces[k] for k in range(PANELS)], axis=1)
    every = lax.all_gather(own, "row", axis=0)
    head = every[:PANELS].reshape(PANELS * block, PANELS * block)
    grid_cols = lax.axis_size("col")
    every = every.reshape(-1, grid_cols, block, PANELS * block)
    gathered = lax.dynamic_index_in_dim(every, mine, 1, keepdims=False)
    return head, own, gathered


def head_of(targets):
    my_row = lax.axis_index("row")
    kept = jnp.concatenate(
        [jnp.where(my_row == k, targets, F32(0.0)) for k in range(PANELS)], axis=0
    )
    return lax.psum(kept, "row")


def shards(matrix, targets):
    rows = lax.axis_size("row")
    if lax.axis_size("col") == PANELS == 2 and rows % 4 == 0 and rows >= 8:
        return fused(matrix, targets)
    head_rhs = head_of(targets)
    head, own, gathered = gather(matrix, targets)
    block = matrix.shape[0]
    width = PANELS * block
    vmem = pl.BlockSpec(memory_space=pltpu.VMEM)
    return pl.pallas_call(
        local_kernel,
        out_shape=(
            jax.ShapeDtypeStruct(matrix.shape, F32),
            jax.ShapeDtypeStruct((block, width), F32),
            jax.ShapeDtypeStruct(targets.shape, F32),
        ),
        in_specs=[vmem] * 6,
        out_specs=(vmem, vmem, vmem),
        scratch_shapes=[pltpu.VMEM((width, width), F32)],
        compiler_params=pltpu.CompilerParams(vmem_limit_bytes=48 * 1024 * 1024),
    )(head, own, head_rhs, matrix, targets, gathered)


def solution(mesh):
    return jax.shard_map(
        shards,
        mesh=mesh,
        in_specs=(P("row", "col"), P("row", None)),
        out_specs=(P("row", "col"), P("row", None), P("row", None)),
        check_vma=False,
    )
```

```python
import functools

import jax
import jax.numpy as jnp
from jax import lax
from jax.experimental import pallas as pl
from jax.experimental.pallas import tpu as pltpu
from jax.sharding import PartitionSpec as P

PANELS = 2
TILE = 128
F32 = jnp.float32
HIGHEST = lax.Precision.HIGHEST
NN = (((1,), (0,)), ((), ()))
NT = (((1,), (1,)), ((), ()))
TN = (((0,), (0,)), ((), ()))


def dot(a, b, dims):
    return lax.dot_general(a, b, dims, precision=HIGHEST, preferred_element_type=F32)


def split(a):
    high = a.astype(jnp.bfloat16)
    return high, (a - high.astype(F32)).astype(jnp.bfloat16)


def dot3(a, b, dims):
    (ah, al), (bh, bl) = a, b
    one = functools.partial(lax.dot_general, dimension_numbers=dims, preferred_element_type=F32)
    return one(ah, bh) + (one(ah, bl) + one(al, bh))


def eliminate(block):
    n = block.shape[0]
    lane = lax.broadcasted_iota(jnp.int32, (8, n), 1)
    sub = lax.broadcasted_iota(jnp.int32, (8, n), 0)
    tiles = [block[8 * t : 8 * t + 8] for t in range(n // 8)]

    def wide(x):
        return jnp.broadcast_to(x, (8, n))

    for p in range(0, n, 4):
        g, s = p // 8, p % 8
        quad = (lane >= p) & (lane < p + 4)
        kept = jnp.where(quad, 0.0, tiles[g])
        columns = [wide(tiles[g][:, p + i : p + i + 1]) for i in range(4)]
        a00, a10, a20, a30 = (wide(columns[0][s + i : s + i + 1]) for i in range(4))
        a11, a21, a31 = (wide(columns[1][s + i : s + i + 1]) for i in range(1, 4))
        a22, a32 = (wide(columns[2][s + i : s + i + 1]) for i in range(2, 4))
        a33 = wide(columns[3][s + 3 : s + 4])
        inv0 = 1.0 / a00
        inv1 = a00 * (1.0 / (a00 * a11 - a10 * a10))
        l10, l20, l30 = a10 * inv0, a20 * inv0, a30 * inv0
        c21, c31 = a21 - a20 * l10, a31 - a30 * l10
        l21, l31 = c21 * inv1, c31 * inv1
        s22 = a22 - l20 * a20 - l21 * c21
        s32 = a32 - l30 * a20 - l31 * c21
        s33 = a33 - l30 * a30 - l31 * c31
        inv2 = 1.0 / s22
        inv3 = s22 * (1.0 / (s22 * s33 - s32 * s32))
        l32 = s32 * inv2
        unit = [jnp.where(lane == p + i, 1.0, wide(kept[s + i : s + i + 1])) for i in range(4)]
        u0 = unit[0]
        u1 = unit[1] - l10 * u0
        u2 = unit[2] - l20 * u0 - l21 * u1
        u3 = unit[3] - l30 * u0 - l31 * u1 - l32 * u2
        for t in range(g, n // 8):
            if t == g:
                c0, c1, c2, c3 = columns
            else:
                c0, c1, c2, c3 = (wide(tiles[t][:, p + i : p + i + 1]) for i in range(4))
            c1 = c1 - c0 * l10
            c2 = c2 - c0 * l20 - c1 * l21
            c3 = c3 - c0 * l30 - c1 * l31 - c2 * l32
            base = kept if t == g else jnp.where(quad, 0.0, tiles[t])
            new = base - (c0 * inv0) * u0 - (c1 * inv1) * u1 - (c2 * inv2) * u2 - (c3 * inv3) * u3
            if t == g:
                new = jnp.where(sub > s + 3, new, tiles[g])
                for i, (u, inv) in enumerate(((u0, inv0), (u1, inv1), (u2, inv2), (u3, inv3))):
                    new = jnp.where(sub == s + i, u * jnp.sqrt(inv), new)
            tiles[t] = new
    return jnp.concatenate(tiles, axis=0)


def factorise(work, between):
    n = work.shape[0]
    rows = lax.broadcasted_iota(jnp.int32, (TILE, TILE), 0)
    cols = lax.broadcasted_iota(jnp.int32, (TILE, TILE), 1)
    diagonal = work[:TILE, :TILE]
    for at in range(0, n, TILE):
        end = at + TILE
        inverse = jnp.where(rows >= cols, eliminate(diagonal), 0.0)
        if end == n:
            if at > 0:
                work[at:end, :at] = dot(inverse, work[at:end, :at], NN)
            work[at:end, at:end] = inverse
            between(at // TILE)
            return
        after = dot(inverse, work[at:end, end:], NN)
        nearest = after[:, :TILE]
        diagonal = work[end : end + TILE, end : end + TILE] - dot(nearest, nearest, TN)
        between(at // TILE)
        work[end:, end:] = work[end:, end:] - dot(after, after, TN)
        work[end:, at:end] = -dot(after, inverse, TN)
        if at > 0:
            before = dot(inverse, work[at:end, :at], NN)
            work[at:end, :at] = before
            work[end:, :at] = work[end:, :at] - dot(after, before, TN)
        work[at:end, at:end] = inverse


def finish(my_row, my_col, work, own, head, head_rhs, matrix, rhs, gathered, out, factor, solved):
    block = matrix.shape[0]
    width = own.shape[1]
    row_id = lax.broadcasted_iota(jnp.int32, (width, width), 0)
    col_id = lax.broadcasted_iota(jnp.int32, (width, width), 1)
    inverse = jnp.where(row_id >= col_id, work[...], 0.0)
    rows = lax.broadcasted_iota(jnp.int32, (block, width), 0) + my_row * block
    cols = lax.broadcasted_iota(jnp.int32, (block, width), 1)
    panel = jnp.where(cols <= rows, dot(own[...], inverse, NT), 0.0)
    factor[...] = panel
    panel = jnp.where(cols < my_row * block, panel, 0.0)
    top = dot(inverse, head_rhs[...], NN)
    value = rhs[...] - dot(panel, top, NN)
    for k in range(width // block):
        value = jnp.where(my_row == k, top[k * block : (k + 1) * block], value)
    solved[...] = value
    weight = dot(panel, inverse, NN)
    first = jnp.where(my_col == 0, 0.0, weight)
    for k in range(1, width // block):
        part = dot(jnp.where(cols < k * block, panel, 0.0), inverse, NN)
        first = jnp.where(my_col == k, part, first)
    first, weight = split(first), split(weight)
    for m in range(matrix.shape[1] // block):
        here = slice(m * block, (m + 1) * block)
        other = gathered[m]
        if m == 0 and head is not None:
            other = head[pl.ds(pl.multiple_of(my_col * block, block), block), :]
        other = split(other)
        out[:, here] = matrix[:, here] - dot3(first if m == 0 else weight, other, NT)


def local_kernel(head, own, head_rhs, matrix, rhs, gathered, out, factor, solved, work):
    work[...] = head[...]
    factorise(work, lambda k: None)
    finish(
        lax.axis_index("row"), lax.axis_index("col"),
        work, own, None, head_rhs, matrix, rhs, gathered, out, factor, solved,
    )


CHUNKS = 4
MESH = pl.DeviceIdType.MESH


def fused_kernel(
    matrix, rhs, out, factor, solved, work, own, head, head_rhs, gathered,
    head_send, head_recv, ring_send, ring_recv, core_send, core_recv, swap_send, swap_recv,
):
    block = matrix.shape[0]
    half, chunk = block // 2, block // CHUNKS
    my_row, col = lax.axis_index("row"), lax.axis_index("col")
    chips = lax.axis_size("row") // 2
    far = chips // 2
    chip, core = my_row // 2, lax.rem(my_row, 2)

    def chip_at(place):
        return jnp.where(place < far, 2 * place, 2 * (chips - 1 - place) + 1)

    place = jnp.where(lax.rem(chip, 2) == 0, chip // 2, chips - 1 - chip // 2)
    right = (2 * chip_at(lax.rem(place + 1, chips)) + core, col)
    left = (2 * chip_at(lax.rem(place + chips - 1, chips)) + core, col)
    sibling = (2 * chip + 1 - core, col)
    across = (my_row, 1 - col)
    cross = (2 * chip + 1 - core, 1 - col)

    def copy(src, dst, send, recv, device):
        return pltpu.make_async_remote_copy(
            src_ref=src, dst_ref=dst, send_sem=send, recv_sem=recv,
            device_id=device, device_id_type=MESH,
        )

    def when(condition, action):
        pl.when(condition)(action)

    def panel_at(index):
        return pl.ds(pl.multiple_of(index * block, block), block)

    def rows_at(index, size):
        return pl.ds(pl.multiple_of(index * size, size), size)

    barrier = pltpu.get_barrier_semaphore()
    for device in (right, left, sibling, across, cross):
        pl.semaphore_signal(barrier, inc=1, device_id=device, device_id_type=MESH)
    pl.semaphore_wait(barrier, 5)

    def head_part(i, on_core, on_col):
        if i == CHUNKS:
            return head_rhs.at[panel_at(on_core), :]
        return head.at[
            pl.ds(pl.multiple_of(on_core * block + i * chunk, chunk), chunk), panel_at(on_col)
        ]

    def head_copy(kind, i, device, on_core, on_col):
        part = head_part(i, on_core, on_col)
        return copy(part, part, head_send.at[kind, i], head_recv.at[kind, i], device)

    def head_right(i):
        part = head_part(i, core, col)
        return copy(part, part, head_send.at[0, i], head_recv.at[0, i], right)

    def head_left(i):
        part = head_part(i, core, col)
        return copy(part, part, head_send.at[1, i], head_recv.at[0, i], left)

    sends_right = place < far
    sends_left = (place == 0) | (place > far + 1)

    @pl.when(place == 0)
    def _():
        head[panel_at(core), panel_at(col)] = matrix[:, :block]
        head_rhs[panel_at(core), :] = rhs[...]

    own[:, panel_at(col)] = matrix[:, :block]
    mine = core == col

    def swap_same():
        here = rows_at(1 - core, half)
        return copy(
            matrix.at[here, pl.ds(0, block)],
            gathered.at[chip, here, panel_at(col)],
            swap_send.at[0], swap_recv.at[0], sibling,
        )

    def swap_over(kind, to_core, device):
        here = rows_at(to_core, half)
        return copy(
            matrix.at[here, pl.ds(0, block)],
            gathered.at[chip, here, panel_at(col)],
            swap_send.at[kind], swap_recv.at[1], device,
        )

    own_copy = copy(
        matrix.at[:, pl.ds(0, block)], own.at[:, panel_at(col)], swap_send.at[3], swap_recv.at[3], across
    )

    for i in range(CHUNKS + 1):
        when(place > 0, lambda i=i: head_right(i).wait_recv())
        when(sends_right, lambda i=i: head_right(i).start())
        when(sends_left, lambda i=i: head_left(i).start())
        if i < CHUNKS:
            head_copy(2, i, across, core, col).start()
        head_copy(3, i, sibling, core, col).start()

    @pl.when(mine)
    def _():
        here = rows_at(core, half)
        gathered[chip, here, panel_at(col)] = matrix[here, :block]
        swap_same().start()

    @pl.when(jnp.logical_not(mine))
    def _():
        swap_over(1, core, across).start()
        swap_over(2, 1 - core, cross).start()

    for i in range(CHUNKS):
        part = head_part(i, core, 1 - col)
        copy(part, part, head_send.at[2, i], head_recv.at[2, i], across).wait_recv()
        head_copy(4, i, sibling, core, 1 - col).start()
    own_copy.start()
    for i in range(CHUNKS):
        for kind, on_col in ((3, col), (4, 1 - col)):
            part = head_part(i, 1 - core, on_col)
            copy(part, part, head_send.at[kind, i], head_recv.at[kind, i], sibling).wait_recv()
    work[...] = head[...]

    def piece(origin, on_core, part=None):
        start, size = on_core * half, half
        if part is not None:
            start, size = start + part * (half // 2), half // 2
        return gathered.at[chip_at(origin), pl.ds(pl.multiple_of(start, size), size), :]

    def origin(direction, step):
        return lax.rem(place + (chips - step if direction == 0 else step), chips)

    def ring_copy(direction, step, source):
        part = direction if step == far else None
        ref = piece(source, core, part)
        return copy(
            ref, ref, ring_send.at[direction, step], ring_recv.at[direction, step],
            left if direction else right,
        )

    def core_copy(index, source, on_core):
        ref = piece(source, on_core)
        return copy(ref, ref, core_send.at[index], core_recv.at[index], sibling)

    def ring_start(step):
        for direction in range(2):
            source = origin(direction, step - 1)
            when(source > 0, lambda d=direction, o=source: ring_copy(d, step, o).start())

    arrivals = [(0, place)] + [
        (1 + direction * (far - 1) + step - 1, origin(direction, step))
        for direction in range(2) for step in range(1, far)
    ] + [(2 * far - 1, origin(0, far))]

    def ring_step(step):
        for direction in range(2):
            source = origin(direction, step)
            when(source > 0, lambda d=direction, o=source: ring_copy(d, step, o).wait_recv())
        if step < far:
            ring_start(step + 1)
            for direction in range(2):
                source = origin(direction, step)
                index = 1 + direction * (far - 1) + step - 1
                when(source > 0, lambda n=index, o=source: core_copy(n, o, core).start())
        else:
            source = origin(0, far)
            when(source > 0, lambda: core_copy(2 * far - 1, source, core).start())

    when(jnp.logical_not(mine), lambda: swap_same().wait_recv())
    swap_over(1, core, across).wait_recv()
    ring_start(1)
    when(place > 0, lambda: core_copy(0, place, core).start())

    steps = work.shape[0] // TILE
    factorise(work, lambda k: [ring_step(s) for s in range(1, far + 1) if min(s, steps) == k + 1])

    for index, source in arrivals:
        when(source > 0, lambda n=index, o=source: core_copy(n, o, 1 - core).wait_recv())
    own_copy.wait_recv()
    part = head_part(CHUNKS, 1 - core, col)
    copy(part, part, head_send.at[3, CHUNKS], head_recv.at[3, CHUNKS], sibling).wait_recv()

    finish(my_row, col, work, own, head, head_rhs, matrix, rhs, gathered, out, factor, solved)

    for i in range(CHUNKS + 1):
        when(sends_right, lambda i=i: head_right(i).wait_send())
        when(sends_left, lambda i=i: head_left(i).wait_send())
        head_copy(3, i, sibling, core, col).wait_send()
        if i < CHUNKS:
            head_copy(2, i, across, core, col).wait_send()
            head_copy(4, i, sibling, core, 1 - col).wait_send()
    when(mine, lambda: swap_same().wait_send())
    for kind, to_core, device in ((1, core, across), (2, 1 - core, cross)):
        when(jnp.logical_not(mine), lambda k=kind, t=to_core, d=device: swap_over(k, t, d).wait_send())
    own_copy.wait_send()
    for step in range(1, far + 1):
        for direction in range(2):
            source = origin(direction, step - 1)
            when(source > 0, lambda d=direction, s=step, o=source: ring_copy(d, s, o).wait_send())
    for index, source in arrivals:
        when(source > 0, lambda n=index, o=source: core_copy(n, o, core).wait_send())


def fused(matrix, targets):
    block = matrix.shape[0]
    width = PANELS * block
    chips = lax.axis_size("row") // 2
    vmem = pl.BlockSpec(memory_space=pltpu.VMEM)
    dma = pltpu.SemaphoreType.DMA
    return pl.pallas_call(
        fused_kernel,
        out_shape=(
            jax.ShapeDtypeStruct(matrix.shape, F32),
            jax.ShapeDtypeStruct((block, width), F32),
            jax.ShapeDtypeStruct(targets.shape, F32),
        ),
        in_specs=[vmem] * 2,
        out_specs=(vmem, vmem, vmem),
        scratch_shapes=[
            pltpu.VMEM((width, width), F32),
            pltpu.VMEM((block, width), F32),
            pltpu.VMEM((width, width), F32),
            pltpu.VMEM((width, targets.shape[1]), F32),
            pltpu.VMEM((chips, block, width), F32),
            dma((5, CHUNKS + 1)), dma((5, CHUNKS + 1)),
            dma((2, chips // 2 + 1)), dma((2, chips // 2 + 1)),
            dma((chips,)), dma((chips,)),
            dma((4,)), dma((4,)),
        ],
        compiler_params=pltpu.CompilerParams(
            vmem_limit_bytes=48 * 1024 * 1024, collective_id=0, has_side_effects=True
        ),
    )(matrix, targets)


def gather(matrix, targets):
    block = matrix.shape[0]
    mine = lax.axis_index("col")
    pieces = lax.all_gather(matrix[:, :block], "col", axis=0)
    own = jnp.concatenate([pieces[k] for k in range(PANELS)], axis=1)
    every = lax.all_gather(own, "row", axis=0)
    head = every[:PANELS].reshape(PANELS * block, PANELS * block)
    grid_cols = lax.axis_size("col")
    every = every.reshape(-1, grid_cols, block, PANELS * block)
    gathered = lax.dynamic_index_in_dim(every, mine, 1, keepdims=False)
    return head, own, gathered


def head_of(targets):
    my_row = lax.axis_index("row")
    kept = jnp.concatenate(
        [jnp.where(my_row == k, targets, F32(0.0)) for k in range(PANELS)], axis=0
    )
    return lax.psum(kept, "row")


def shards(matrix, targets):
    rows = lax.axis_size("row")
    if lax.axis_size("col") == PANELS == 2 and rows % 4 == 0 and rows >= 8:
        return fused(matrix, targets)
    head_rhs = head_of(targets)
    head, own, gathered = gather(matrix, targets)
    block = matrix.shape[0]
    width = PANELS * block
    vmem = pl.BlockSpec(memory_space=pltpu.VMEM)
    return pl.pallas_call(
        local_kernel,
        out_shape=(
            jax.ShapeDtypeStruct(matrix.shape, F32),
            jax.ShapeDtypeStruct((block, width), F32),
            jax.ShapeDtypeStruct(targets.shape, F32),
        ),
        in_specs=[vmem] * 6,
        out_specs=(vmem, vmem, vmem),
        scratch_shapes=[pltpu.VMEM((width, width), F32)],
        compiler_params=pltpu.CompilerParams(vmem_limit_bytes=48 * 1024 * 1024),
    )(head, own, head_rhs, matrix, targets, gathered)


def solution(mesh):
    return jax.shard_map(
        shards,
        mesh=mesh,
        in_specs=(P("row", "col"), P("row", None)),
        out_specs=(P("row", "col"), P("row", None), P("row", None)),
        check_vma=False,
    )
```

```python
import functools

import jax
import jax.numpy as jnp
from jax import lax
from jax.experimental import pallas as pl
from jax.experimental.pallas import tpu as pltpu
from jax.sharding import PartitionSpec as P

PANELS = 2
TILE = 128
STRIP = 32
F32 = jnp.float32
HIGHEST = lax.Precision.HIGHEST
NN = (((1,), (0,)), ((), ()))
NT = (((1,), (1,)), ((), ()))
TN = (((0,), (0,)), ((), ()))


def dot(a, b, dims):
    return lax.dot_general(a, b, dims, precision=HIGHEST, preferred_element_type=F32)


def split(a):
    high = a.astype(jnp.bfloat16)
    return high, (a - high.astype(F32)).astype(jnp.bfloat16)


def dot3(a, b, dims):
    (ah, al), (bh, bl) = a, b
    one = functools.partial(lax.dot_general, dimension_numbers=dims, preferred_element_type=F32)
    return one(ah, bh) + (one(ah, bl) + one(al, bh))


def eliminate(block):
    n = block.shape[0]
    lane = lax.broadcasted_iota(jnp.int32, (STRIP, n), 1)
    row = lax.broadcasted_iota(jnp.int32, (STRIP, n), 0)
    strips = []
    below = block
    for at in range(0, n, STRIP):
        strip = eliminate_strip(below[:STRIP], at)
        strips.append(strip)
        if at + STRIP < n:
            inside = (lane >= at) & (lane < at + STRIP)
            right = jnp.where(inside & (lane > at + row), 0.0, strip)
            rest = n - at - STRIP
            wide_lane = lax.broadcasted_iota(jnp.int32, (rest, n), 1)
            cleared = jnp.where((wide_lane >= at) & (wide_lane < at + STRIP), 0.0, below[STRIP:])
            below = cleared - dot(strip, right, TN)[at + STRIP :]
    return jnp.concatenate(strips, axis=0)


def eliminate_strip(strip, at):
    n = strip.shape[1]
    lane = lax.broadcasted_iota(jnp.int32, (8, n), 1)
    sub = lax.broadcasted_iota(jnp.int32, (8, n), 0)
    tiles = [strip[8 * t : 8 * t + 8] for t in range(STRIP // 8)]

    def wide(x):
        return jnp.broadcast_to(x, (8, n))

    for p in range(at, at + STRIP, 4):
        g, s = (p - at) // 8, p % 8
        quad = (lane >= p) & (lane < p + 4)
        kept = jnp.where(quad, 0.0, tiles[g])
        columns = [wide(tiles[g][:, p + i : p + i + 1]) for i in range(4)]
        a00, a10, a20, a30 = (wide(columns[0][s + i : s + i + 1]) for i in range(4))
        a11, a21, a31 = (wide(columns[1][s + i : s + i + 1]) for i in range(1, 4))
        a22, a32 = (wide(columns[2][s + i : s + i + 1]) for i in range(2, 4))
        a33 = wide(columns[3][s + 3 : s + 4])
        inv0 = 1.0 / a00
        inv1 = a00 * (1.0 / (a00 * a11 - a10 * a10))
        l10, l20, l30 = a10 * inv0, a20 * inv0, a30 * inv0
        c21, c31 = a21 - a20 * l10, a31 - a30 * l10
        l21, l31 = c21 * inv1, c31 * inv1
        s22 = a22 - l20 * a20 - l21 * c21
        s32 = a32 - l30 * a20 - l31 * c21
        s33 = a33 - l30 * a30 - l31 * c31
        inv2 = 1.0 / s22
        inv3 = s22 * (1.0 / (s22 * s33 - s32 * s32))
        l32 = s32 * inv2
        unit = [jnp.where(lane == p + i, 1.0, wide(kept[s + i : s + i + 1])) for i in range(4)]
        u0 = unit[0]
        u1 = unit[1] - l10 * u0
        u2 = unit[2] - l20 * u0 - l21 * u1
        u3 = unit[3] - l30 * u0 - l31 * u1 - l32 * u2
        for t in range(g, STRIP // 8):
            if t == g:
                c0, c1, c2, c3 = columns
            else:
                c0, c1, c2, c3 = (wide(tiles[t][:, p + i : p + i + 1]) for i in range(4))
            c1 = c1 - c0 * l10
            c2 = c2 - c0 * l20 - c1 * l21
            c3 = c3 - c0 * l30 - c1 * l31 - c2 * l32
            base = kept if t == g else jnp.where(quad, 0.0, tiles[t])
            new = base - (c0 * inv0) * u0 - (c1 * inv1) * u1 - (c2 * inv2) * u2 - (c3 * inv3) * u3
            if t == g:
                new = jnp.where(sub > s + 3, new, tiles[g])
                for i, (u, inv) in enumerate(((u0, inv0), (u1, inv1), (u2, inv2), (u3, inv3))):
                    new = jnp.where(sub == s + i, u * jnp.sqrt(inv), new)
            tiles[t] = new
    return jnp.concatenate(tiles, axis=0)


def factorise(work, between):
    n = work.shape[0]
    rows = lax.broadcasted_iota(jnp.int32, (TILE, TILE), 0)
    cols = lax.broadcasted_iota(jnp.int32, (TILE, TILE), 1)
    diagonal = work[:TILE, :TILE]
    for at in range(0, n, TILE):
        end = at + TILE
        inverse = jnp.where(rows >= cols, eliminate(diagonal), 0.0)
        if end == n:
            if at > 0:
                work[at:end, :at] = dot(inverse, work[at:end, :at], NN)
            work[at:end, at:end] = inverse
            between(at // TILE)
            return
        after = dot(inverse, work[at:end, end:], NN)
        nearest = after[:, :TILE]
        diagonal = work[end : end + TILE, end : end + TILE] - dot(nearest, nearest, TN)
        between(at // TILE)
        work[end:, end:] = work[end:, end:] - dot(after, after, TN)
        work[end:, at:end] = -dot(after, inverse, TN)
        if at > 0:
            before = dot(inverse, work[at:end, :at], NN)
            work[at:end, :at] = before
            work[end:, :at] = work[end:, :at] - dot(after, before, TN)
        work[at:end, at:end] = inverse


def finish(my_row, my_col, work, own, head, head_rhs, matrix, rhs, gathered, out, factor, solved):
    block = matrix.shape[0]
    width = own.shape[1]
    row_id = lax.broadcasted_iota(jnp.int32, (width, width), 0)
    col_id = lax.broadcasted_iota(jnp.int32, (width, width), 1)
    inverse = jnp.where(row_id >= col_id, work[...], 0.0)
    rows = lax.broadcasted_iota(jnp.int32, (block, width), 0) + my_row * block
    cols = lax.broadcasted_iota(jnp.int32, (block, width), 1)
    panel = jnp.where(cols <= rows, dot(own[...], inverse, NT), 0.0)
    factor[...] = panel
    panel = jnp.where(cols < my_row * block, panel, 0.0)
    top = dot(inverse, head_rhs[...], NN)
    value = rhs[...] - dot(panel, top, NN)
    for k in range(width // block):
        value = jnp.where(my_row == k, top[k * block : (k + 1) * block], value)
    solved[...] = value
    weight = dot(panel, inverse, NN)
    first = jnp.where(my_col == 0, 0.0, weight)
    for k in range(1, width // block):
        part = dot(jnp.where(cols < k * block, panel, 0.0), inverse, NN)
        first = jnp.where(my_col == k, part, first)
    first, weight = split(first), split(weight)
    for m in range(matrix.shape[1] // block):
        here = slice(m * block, (m + 1) * block)
        other = gathered[m]
        if m == 0 and head is not None:
            other = head[pl.ds(pl.multiple_of(my_col * block, block), block), :]
        other = split(other)
        out[:, here] = matrix[:, here] - dot3(first if m == 0 else weight, other, NT)


def local_kernel(head, own, head_rhs, matrix, rhs, gathered, out, factor, solved, work):
    work[...] = head[...]
    factorise(work, lambda k: None)
    finish(
        lax.axis_index("row"), lax.axis_index("col"),
        work, own, None, head_rhs, matrix, rhs, gathered, out, factor, solved,
    )


CHUNKS = 4
MESH = pl.DeviceIdType.MESH


def fused_kernel(
    matrix, rhs, out, factor, solved, work, own, head, head_rhs, gathered,
    head_send, head_recv, ring_send, ring_recv, core_send, core_recv, swap_send, swap_recv,
):
    block = matrix.shape[0]
    half, chunk = block // 2, block // CHUNKS
    my_row, col = lax.axis_index("row"), lax.axis_index("col")
    chips = lax.axis_size("row") // 2
    far = chips // 2
    chip, core = my_row // 2, lax.rem(my_row, 2)

    def chip_at(place):
        return jnp.where(place < far, 2 * place, 2 * (chips - 1 - place) + 1)

    place = jnp.where(lax.rem(chip, 2) == 0, chip // 2, chips - 1 - chip // 2)
    right = (2 * chip_at(lax.rem(place + 1, chips)) + core, col)
    left = (2 * chip_at(lax.rem(place + chips - 1, chips)) + core, col)
    sibling = (2 * chip + 1 - core, col)
    across = (my_row, 1 - col)
    cross = (2 * chip + 1 - core, 1 - col)

    def copy(src, dst, send, recv, device):
        return pltpu.make_async_remote_copy(
            src_ref=src, dst_ref=dst, send_sem=send, recv_sem=recv,
            device_id=device, device_id_type=MESH,
        )

    def when(condition, action):
        pl.when(condition)(action)

    def panel_at(index):
        return pl.ds(pl.multiple_of(index * block, block), block)

    def rows_at(index, size):
        return pl.ds(pl.multiple_of(index * size, size), size)

    barrier = pltpu.get_barrier_semaphore()
    for device in (right, left, sibling, across, cross):
        pl.semaphore_signal(barrier, inc=1, device_id=device, device_id_type=MESH)
    pl.semaphore_wait(barrier, 5)

    def head_part(i, on_core, on_col):
        if i == CHUNKS:
            return head_rhs.at[panel_at(on_core), :]
        return head.at[
            pl.ds(pl.multiple_of(on_core * block + i * chunk, chunk), chunk), panel_at(on_col)
        ]

    def head_copy(kind, i, device, on_core, on_col):
        part = head_part(i, on_core, on_col)
        return copy(part, part, head_send.at[kind, i], head_recv.at[kind, i], device)

    def head_right(i):
        part = head_part(i, core, col)
        return copy(part, part, head_send.at[0, i], head_recv.at[0, i], right)

    def head_left(i):
        part = head_part(i, core, col)
        return copy(part, part, head_send.at[1, i], head_recv.at[0, i], left)

    sends_right = place < far
    sends_left = (place == 0) | (place > far + 1)

    @pl.when(place == 0)
    def _():
        head[panel_at(core), panel_at(col)] = matrix[:, :block]
        head_rhs[panel_at(core), :] = rhs[...]

    own[:, panel_at(col)] = matrix[:, :block]
    mine = core == col

    def swap_same():
        here = rows_at(1 - core, half)
        return copy(
            matrix.at[here, pl.ds(0, block)],
            gathered.at[chip, here, panel_at(col)],
            swap_send.at[0], swap_recv.at[0], sibling,
        )

    def swap_over(kind, to_core, device):
        here = rows_at(to_core, half)
        return copy(
            matrix.at[here, pl.ds(0, block)],
            gathered.at[chip, here, panel_at(col)],
            swap_send.at[kind], swap_recv.at[1], device,
        )

    own_copy = copy(
        matrix.at[:, pl.ds(0, block)], own.at[:, panel_at(col)], swap_send.at[3], swap_recv.at[3], across
    )

    for i in range(CHUNKS + 1):
        when(place > 0, lambda i=i: head_right(i).wait_recv())
        when(sends_right, lambda i=i: head_right(i).start())
        when(sends_left, lambda i=i: head_left(i).start())
        if i < CHUNKS:
            head_copy(2, i, across, core, col).start()
        head_copy(3, i, sibling, core, col).start()

    @pl.when(mine)
    def _():
        here = rows_at(core, half)
        gathered[chip, here, panel_at(col)] = matrix[here, :block]
        swap_same().start()

    @pl.when(jnp.logical_not(mine))
    def _():
        swap_over(1, core, across).start()
        swap_over(2, 1 - core, cross).start()

    for i in range(CHUNKS):
        part = head_part(i, core, 1 - col)
        copy(part, part, head_send.at[2, i], head_recv.at[2, i], across).wait_recv()
        head_copy(4, i, sibling, core, 1 - col).start()
    own_copy.start()
    for i in range(CHUNKS):
        for kind, on_col in ((3, col), (4, 1 - col)):
            part = head_part(i, 1 - core, on_col)
            copy(part, part, head_send.at[kind, i], head_recv.at[kind, i], sibling).wait_recv()
    work[...] = head[...]

    def piece(origin, on_core, part=None):
        start, size = on_core * half, half
        if part is not None:
            start, size = start + part * (half // 2), half // 2
        return gathered.at[chip_at(origin), pl.ds(pl.multiple_of(start, size), size), :]

    def origin(direction, step):
        return lax.rem(place + (chips - step if direction == 0 else step), chips)

    def ring_copy(direction, step, source):
        part = direction if step == far else None
        ref = piece(source, core, part)
        return copy(
            ref, ref, ring_send.at[direction, step], ring_recv.at[direction, step],
            left if direction else right,
        )

    def core_copy(index, source, on_core):
        ref = piece(source, on_core)
        return copy(ref, ref, core_send.at[index], core_recv.at[index], sibling)

    def ring_start(step):
        for direction in range(2):
            source = origin(direction, step - 1)
            when(source > 0, lambda d=direction, o=source: ring_copy(d, step, o).start())

    arrivals = [(0, place)] + [
        (1 + direction * (far - 1) + step - 1, origin(direction, step))
        for direction in range(2) for step in range(1, far)
    ] + [(2 * far - 1, origin(0, far))]

    def ring_step(step):
        for direction in range(2):
            source = origin(direction, step)
            when(source > 0, lambda d=direction, o=source: ring_copy(d, step, o).wait_recv())
        if step < far:
            ring_start(step + 1)
            for direction in range(2):
                source = origin(direction, step)
                index = 1 + direction * (far - 1) + step - 1
                when(source > 0, lambda n=index, o=source: core_copy(n, o, core).start())
        else:
            source = origin(0, far)
            when(source > 0, lambda: core_copy(2 * far - 1, source, core).start())

    when(jnp.logical_not(mine), lambda: swap_same().wait_recv())
    swap_over(1, core, across).wait_recv()
    ring_start(1)
    when(place > 0, lambda: core_copy(0, place, core).start())

    steps = work.shape[0] // TILE
    factorise(work, lambda k: [ring_step(s) for s in range(1, far + 1) if min(s, steps) == k + 1])

    for index, source in arrivals:
        when(source > 0, lambda n=index, o=source: core_copy(n, o, 1 - core).wait_recv())
    own_copy.wait_recv()
    part = head_part(CHUNKS, 1 - core, col)
    copy(part, part, head_send.at[3, CHUNKS], head_recv.at[3, CHUNKS], sibling).wait_recv()

    finish(my_row, col, work, own, head, head_rhs, matrix, rhs, gathered, out, factor, solved)

    for i in range(CHUNKS + 1):
        when(sends_right, lambda i=i: head_right(i).wait_send())
        when(sends_left, lambda i=i: head_left(i).wait_send())
        head_copy(3, i, sibling, core, col).wait_send()
        if i < CHUNKS:
            head_copy(2, i, across, core, col).wait_send()
            head_copy(4, i, sibling, core, 1 - col).wait_send()
    when(mine, lambda: swap_same().wait_send())
    for kind, to_core, device in ((1, core, across), (2, 1 - core, cross)):
        when(jnp.logical_not(mine), lambda k=kind, t=to_core, d=device: swap_over(k, t, d).wait_send())
    own_copy.wait_send()
    for step in range(1, far + 1):
        for direction in range(2):
            source = origin(direction, step - 1)
            when(source > 0, lambda d=direction, s=step, o=source: ring_copy(d, s, o).wait_send())
    for index, source in arrivals:
        when(source > 0, lambda n=index, o=source: core_copy(n, o, core).wait_send())


def fused(matrix, targets):
    block = matrix.shape[0]
    width = PANELS * block
    chips = lax.axis_size("row") // 2
    vmem = pl.BlockSpec(memory_space=pltpu.VMEM)
    dma = pltpu.SemaphoreType.DMA
    return pl.pallas_call(
        fused_kernel,
        out_shape=(
            jax.ShapeDtypeStruct(matrix.shape, F32),
            jax.ShapeDtypeStruct((block, width), F32),
            jax.ShapeDtypeStruct(targets.shape, F32),
        ),
        in_specs=[vmem] * 2,
        out_specs=(vmem, vmem, vmem),
        scratch_shapes=[
            pltpu.VMEM((width, width), F32),
            pltpu.VMEM((block, width), F32),
            pltpu.VMEM((width, width), F32),
            pltpu.VMEM((width, targets.shape[1]), F32),
            pltpu.VMEM((chips, block, width), F32),
            dma((5, CHUNKS + 1)), dma((5, CHUNKS + 1)),
            dma((2, chips // 2 + 1)), dma((2, chips // 2 + 1)),
            dma((chips,)), dma((chips,)),
            dma((4,)), dma((4,)),
        ],
        compiler_params=pltpu.CompilerParams(
            vmem_limit_bytes=48 * 1024 * 1024, collective_id=0, has_side_effects=True
        ),
    )(matrix, targets)


def gather(matrix, targets):
    block = matrix.shape[0]
    mine = lax.axis_index("col")
    pieces = lax.all_gather(matrix[:, :block], "col", axis=0)
    own = jnp.concatenate([pieces[k] for k in range(PANELS)], axis=1)
    every = lax.all_gather(own, "row", axis=0)
    head = every[:PANELS].reshape(PANELS * block, PANELS * block)
    grid_cols = lax.axis_size("col")
    every = every.reshape(-1, grid_cols, block, PANELS * block)
    gathered = lax.dynamic_index_in_dim(every, mine, 1, keepdims=False)
    return head, own, gathered


def head_of(targets):
    my_row = lax.axis_index("row")
    kept = jnp.concatenate(
        [jnp.where(my_row == k, targets, F32(0.0)) for k in range(PANELS)], axis=0
    )
    return lax.psum(kept, "row")


def shards(matrix, targets):
    rows = lax.axis_size("row")
    if lax.axis_size("col") == PANELS == 2 and rows % 4 == 0 and rows >= 8:
        return fused(matrix, targets)
    head_rhs = head_of(targets)
    head, own, gathered = gather(matrix, targets)
    block = matrix.shape[0]
    width = PANELS * block
    vmem = pl.BlockSpec(memory_space=pltpu.VMEM)
    return pl.pallas_call(
        local_kernel,
        out_shape=(
            jax.ShapeDtypeStruct(matrix.shape, F32),
            jax.ShapeDtypeStruct((block, width), F32),
            jax.ShapeDtypeStruct(targets.shape, F32),
        ),
        in_specs=[vmem] * 6,
        out_specs=(vmem, vmem, vmem),
        scratch_shapes=[pltpu.VMEM((width, width), F32)],
        compiler_params=pltpu.CompilerParams(vmem_limit_bytes=48 * 1024 * 1024),
    )(head, own, head_rhs, matrix, targets, gathered)


def solution(mesh):
    return jax.shard_map(
        shards,
        mesh=mesh,
        in_specs=(P("row", "col"), P("row", None)),
        out_specs=(P("row", "col"), P("row", None), P("row", None)),
        check_vma=False,
    )
```
